256 devices in a mesh: dp: 4 (over y), cache: 8 (over x, core), tensor: 8 (over z).
Axes of the slice: x: 4, y: 4, z: 8, core: 2. Of those that a mesh axis runs over, the one named last changes fastest.
Arguments:
- queries: bfloat16 [32, 256, 16384], P(('dp', 'cache'), None, 'tensor'), may hold values from -6 to 6
- suffix_keys: bfloat16 [32, 256, 1024], P(('dp', 'cache'), None, 'tensor'), may hold values from -12 to 12
- suffix_values: bfloat16 [32, 256, 1024], P(('dp', 'cache'), None, 'tensor'), may hold values from -16 to 16
- prefix_keys: bfloat16 [32, 32, 128, 1024], P(('dp', 'cache'), None, None, 'tensor'), may hold values from -12 to 12
- prefix_values: bfloat16 [32, 32, 128, 1024], P(('dp', 'cache'), None, None, 'tensor'), may hold values from -16 to 16
- hit_len: int32 [32], replicated, may hold values from 1 to 4096, 65536 in all
- suffix_len: int32 [32], replicated, may hold values from 1 to 256, 4096 in all
- page_map: int32 [32, 32], replicated, may hold values from 0 to 31, each once within a row
Outputs:
- attended: bfloat16 [32, 256, 16384], P(('dp', 'cache'), 'tensor')
The draws below stay inside these ranges and needn't reach their ends.
Inputs may be any that keep to these rules, and one draw needn't show every extreme that they name: Each row of page_map names every holder once: the device of dp+cache with index page_map[r, p] holds page p of request r, at slot r of its prefix arrays.
All inputs are finite; a program needn't handle non-finite values.
Results may differ from the reference program's by a relative error of at most 0.006.
Values may be sent and summed in bfloat16 or wider, within the bound.
No kernel may reach another device: no remote copies, remote signals or barrier semaphores. Data moves between devices by JAX's collectives and lax.ppermute only.
A program may use at most 64 MiB of HBM per device.

```python
import math
import jax
import jax.numpy as jnp
import numpy as np
from jax import lax

H = 128
KVH = 8
HD = 128
PAGE = 128
SUF = 256
GROUP = 32
REQS = 32


def draw_queries(key, part):
    key = jax.random.fold_in(key, 1)
    base = jax.random.truncated_normal(key, -6.0, 6.0, (REQS, SUF, H * HD), jnp.float32)
    return base.astype(jnp.bfloat16)


def draw_prefix_keys(key, part):
    key = jax.random.fold_in(key, 2)
    base = 2.0 * jax.random.truncated_normal(key, -6.0, 6.0, (GROUP, REQS, PAGE, KVH * HD), jnp.float32)
    return base.astype(jnp.bfloat16)


def draw_suffix_keys(key, part):
    key = jax.random.fold_in(key, 3)
    base = 2.0 * jax.random.truncated_normal(key, -6.0, 6.0, (REQS, SUF, KVH * HD), jnp.float32)
    return base.astype(jnp.bfloat16)


def level_of(stream_key, extent, split, smallest, largest):
    gain, own = 1.0, jax.random.fold_in(stream_key, 6)
    for axis_at, parts in split:
        heights = jnp.exp(jax.random.uniform(jax.random.fold_in(own, axis_at), (parts,), jnp.float32, smallest / len(split), largest / len(split)))
        gain = gain * jnp.repeat(heights, extent[axis_at] // parts).reshape([-1 if axis == axis_at else 1 for axis in range(len(extent))])
    return gain


def split_up(amount, total, limit, skew):
    portions = [(1 << 20) // math.isqrt(grade ** skew) + 1 for grade in range(2, amount + 1)]
    spare, given = total - limit - (amount - 1), [1] * (amount - 1)
    while spare > 0:
        free = [i for i in range(amount - 1) if given[i] < limit]
        mass, left = sum([portions[i] for i in free]), spare
        for i in free:
            extra = min(limit - given[i], max(1, left * portions[i] // mass), spare)
            given[i] = given[i] + extra
            spare = spare - extra
    return np.array([limit] + given)


def uneven_parts(rng, number_of, total, reach, skew):
    if number_of == 2:
        one = jax.random.randint(rng, (), max(1, total - reach), min(reach, total - 1) + 1)
        return jnp.stack([one, total - one])
    lengths = jnp.asarray(split_up(number_of, total, reach, skew), jnp.int32)
    couples = (number_of - 1) // 2
    donor, sink = lengths[1:1 + 2 * couples:2], lengths[2:2 + 2 * couples:2]
    slack = jnp.minimum(donor - 1, reach - sink)
    moved = jax.random.randint(jax.random.fold_in(rng, 1), (couples,), 0, 1 << 20) % (slack + 1)
    lengths = lengths.at[1:1 + 2 * couples:2].set(donor - moved).at[2:2 + 2 * couples:2].set(sink + moved)
    return lengths[jax.random.permutation(jax.random.fold_in(rng, 2), number_of)]


def gaussian(rng, shape, spread, limit, pieces=(), kind=jnp.bfloat16):
    entries = spread * jax.random.normal(rng, shape, jnp.float32)
    if pieces:
        entries = entries * level_of(rng, shape, pieces, -0.22, 0.18)
    return jnp.clip(entries, -limit, limit).astype(kind)


def setup_inputs(seed: int = 0) -> dict:
    streams_of = jax.random.split(jax.random.key(seed), 9)
    queries = draw_queries(jax.random.fold_in(streams_of[8], 71), 0)
    suffix_keys = draw_suffix_keys(jax.random.fold_in(streams_of[8], 71), 0)
    suffix_values = gaussian(streams_of[2], (REQS, SUF, KVH * HD), 3.0, 16.0, ((0, 32), (2, 8)))
    prefix_keys = draw_prefix_keys(jax.random.fold_in(streams_of[8], 71), 0)
    prefix_values = gaussian(streams_of[4], (GROUP, REQS, PAGE, KVH * HD), 3.0, 16.0, ((0, 32), (3, 8)))
    hit_len = uneven_parts(streams_of[5], REQS, REQS * GROUP * PAGE // 2, GROUP * PAGE, 2).astype(jnp.int32)
    suffix_len = uneven_parts(streams_of[6], REQS, REQS * SUF // 2, SUF, 2).astype(jnp.int32)
    page_map = jax.vmap(lambda own: jax.random.permutation(own, GROUP))(jax.random.split(streams_of[7], REQS)).reshape((REQS, GROUP)).astype(jnp.int32)
    return dict(queries=queries, suffix_keys=suffix_keys, suffix_values=suffix_values, prefix_keys=prefix_keys, prefix_values=prefix_values, hit_len=hit_len, suffix_len=suffix_len, page_map=page_map)


def reference(queries, suffix_keys, suffix_values, prefix_keys, prefix_values, hit_len, suffix_len, page_map):
    score_scale = 1.0 / math.sqrt(HD)
    group_size = H // KVH
    holder_ids = jnp.arange(GROUP, dtype=jnp.int32)
    slot_ids = jnp.arange(PAGE, dtype=jnp.int32)
    positions = jnp.arange(SUF, dtype=jnp.int32)

    def per_request(request):
        query_lattice = queries[request].astype(jnp.float32).reshape(SUF, KVH, group_size, HD)
        route_row = page_map[request]
        holder_match = (route_row[None, :] == holder_ids[:, None]).astype(jnp.int32)
        page_index = lax.optimization_barrier(jnp.sum(holder_match * holder_ids[None, :], axis=1))
        key_position = (page_index[:, None] * PAGE + slot_ids[None, :]).reshape(GROUP * PAGE)
        prefix_valid = key_position < hit_len[request]
        causal_mask = positions[None, :] <= positions[:, None]
        key_valid = jnp.concatenate([jnp.broadcast_to(prefix_valid[None, :], (SUF, GROUP * PAGE)), causal_mask], axis=1)
        all_keys = jnp.concatenate([prefix_keys[:, request].reshape(GROUP * PAGE, KVH, HD), suffix_keys[request].reshape(SUF, KVH, HD)], axis=0).astype(jnp.float32)
        all_values = jnp.concatenate([prefix_values[:, request].reshape(GROUP * PAGE, KVH, HD), suffix_values[request].reshape(SUF, KVH, HD)], axis=0).astype(jnp.float32)

        def per_head(head_index):
            head_queries = query_lattice[:, head_index]
            head_keys = all_keys[:, head_index]
            head_values = all_values[:, head_index]
            scores = jnp.einsum('igd,jd->igj', head_queries, head_keys, precision=lax.Precision.HIGHEST) * score_scale
            scores = jnp.where(key_valid[:, None, :], scores, -jnp.inf)
            row_best = lax.optimization_barrier(jnp.max(scores, axis=-1, keepdims=True))
            exp_weights = jnp.exp(scores - row_best)
            row_total = lax.optimization_barrier(jnp.sum(exp_weights, axis=-1))
            attention_weights = lax.optimization_barrier(exp_weights.astype(jnp.bfloat16)).astype(jnp.float32)
            summed = jnp.einsum('igj,jd->igd', attention_weights, head_values, precision=lax.Precision.HIGHEST)
            return summed / row_total[..., None]
        head_out = lax.map(per_head, jnp.arange(KVH, dtype=jnp.int32))
        result = jnp.transpose(head_out, (1, 0, 2, 3)).reshape(SUF, H * HD)
        live_rows = positions < suffix_len[request]
        result = jnp.where(live_rows[:, None], result, jnp.zeros_like(result))
        return result.astype(jnp.bfloat16)
    return lax.map(per_request, jnp.arange(REQS, dtype=jnp.int32))
```

```python
import functools
import math

import jax
import jax.numpy as jnp
from jax import lax
from jax.experimental import pallas as pl
from jax.experimental.pallas import tpu as pltpu
from jax.sharding import PartitionSpec as P

HD = 128
HEADS = 16
WIDTH = HEADS * HD
PAGE = 128
SUF = 256
ROWS = 32
RB = ROWS * HEADS
TILE = 1024
RS = 256
SHIFTS = (4, 3, 5, 2, 6, 1, 7, 0)
PAIRS = (
    ((1, 1), (3, 3)),
    ((1, 3), (3, 1)),
    ((1, 2), (3, 2)),
    ((2, 1), (2, 3)),
    ((0, 1), (0, 3)),
    ((1, 0), (3, 0)),
)
TIES = ((2, 2), (0, 2), (2, 0))
EARLY = 2
HALF = 16
SCALE = math.log2(math.e) / math.sqrt(HD)
F32 = jnp.float32
BF16 = jnp.bfloat16
GROUP = ("dp", "cache")
PARAMS = pltpu.CompilerParams(vmem_limit_bytes=24 << 20)
SMEM = pl.BlockSpec(memory_space=pltpu.SMEM)
VMEM = pl.BlockSpec(memory_space=pltpu.VMEM)


def cost(flops, moved):
    return pl.CostEstimate(flops=flops, transcendentals=flops // 512, bytes_accessed=moved)


def qk(a, b):
    return lax.dot_general(a, b, (((1,), (1,)), ((), ())), preferred_element_type=F32)


def pv(a, b):
    return lax.dot_general(a, b, (((1,), (0,)), ((), ())), preferred_element_type=F32)


def pack_kernel(place, k_ref, v_ref, x_ref, o_ref, t0_ref, t1_ref, t2_ref, own_ref):
    y, x, c = place[0], place[1], place[2]

    def put(dst, index, dy, dx, core):
        r = lax.rem(y + dy, 4) * 8 + lax.rem(x + dx, 4) * 2 + core
        dst[index + (0,)] = k_ref[r]
        dst[index + (1,)] = v_ref[r]

    for j, ((ay, ax), (by, bx)) in enumerate(PAIRS):
        mine = (jnp.where(c == 0, ay, by), jnp.where(c == 0, ax, bx))
        other = (jnp.where(c == 0, by, ay), jnp.where(c == 0, bx, ax))
        for rel in range(2):
            put(x_ref, (2 * j + rel,), *other, (1 - c) ^ rel)
            put(o_ref, (j, rel), *mine, c ^ rel)
    put(x_ref, (2 * len(PAIRS),), 0, 0, 1 - c)
    for (dy, dx), ref in zip(TIES, (t0_ref, t1_ref, t2_ref)):
        for rel in range(2):
            put(ref, (rel,), dy, dx, c ^ rel)
    put(own_ref, (), 0, 0, c)


def join_kernel(o_ref, x_ref, *out_refs):
    for j, ref in enumerate(out_refs):
        ref[0] = o_ref[j]
        ref[1] = x_ref[2 * j:2 * j + 2]


def row_block(q_ref, t):
    q = jnp.concatenate([q_ref[t, :, n * HD:(n + 1) * HD] for n in range(HEADS)], axis=0)
    scaled = q.astype(F32) * SCALE
    high = scaled.astype(BF16)
    low = (scaled - high.astype(F32)).astype(BF16)
    return jnp.concatenate([high, low], axis=1)


def prepare(limits, start, pages, sk_ref, k_out, v_out):
    first_key = sk_ref[0:1, :].astype(F32)
    slot = lax.broadcasted_iota(jnp.int32, (PAGE, HD), 0)
    for i, page in enumerate(pages):
        valid = slot < limits[start + i]
        rows = slice(i * PAGE, (i + 1) * PAGE)
        k_out[rows, :] = jnp.where(valid, page[0].astype(F32), first_key).astype(BF16)
        v_out[rows, :HD] = jnp.where(valid, page[1].astype(F32), 0.0).astype(BF16)
        v_out[rows, HD:] = jnp.where(valid, 1.0, 0.0).astype(BF16)


def attend(q, k_ref, v_ref, best, accum):
    units = [(r, j) for j in range(HALF * PAGE // TILE) for r in range(RB // RS)]

    def score(unit):
        r, j = unit
        k = k_ref[j * TILE:(j + 1) * TILE, :]
        return qk(q[r * RS:(r + 1) * RS], jnp.concatenate([k, k], axis=1))

    ahead = score(units[0])
    for i, (r, j) in enumerate(units):
        s = ahead
        if i + 1 < len(units):
            ahead = score(units[i + 1])
        new = jnp.maximum(best[r], jnp.max(s, axis=1, keepdims=True))
        p = jnp.exp2(s - new).astype(BF16)
        accum[r] = accum[r] * jnp.exp2(best[r] - new) + pv(p, v_ref[j * TILE:(j + 1) * TILE, :])
        best[r] = new
    return best, accum


def first_kernel(place, limits, q_ref, sk_ref, sv_ref, own, x, t0, t1, t2, p0, p1, ya, m_ref, a_ref, k_sc, v_sc):
    pages = [own, x.at[2 * len(PAIRS)], t0.at[0], t1.at[0], t2.at[0]]
    pages += [p.at[src, 0] for p in (p0, p1) for src in range(2)]
    pages += [ya.at[i] for i in range(7)]
    prepare(limits, 0, pages, sk_ref, k_sc, v_sc)
    live = place[4]

    def block(t, _):
        @pl.when(t * ROWS < live)
        def _():
            q = row_block(q_ref, t)
            sk = jnp.concatenate([sk_ref[...]] * 2, axis=1)
            sv = jnp.concatenate([sv_ref[...], jnp.ones((SUF, HD), BF16)], axis=1)
            slot = t * ROWS + lax.broadcasted_iota(jnp.int32, (RS, SUF), 0) % ROWS
            causal = lax.broadcasted_iota(jnp.int32, (RS, SUF), 1) <= slot
            best, accum = [], []
            for r in range(RB // RS):
                s = jnp.where(causal, qk(q[r * RS:(r + 1) * RS], sk), -jnp.inf)
                top = jnp.max(s, axis=1, keepdims=True)
                best.append(top)
                accum.append(pv(jnp.exp2(s - top).astype(BF16), sv))
            best, accum = attend(q, k_sc, v_sc, best, accum)
            for r in range(RB // RS):
                rows = slice(r * RS, (r + 1) * RS)
                m_ref[t, rows, :] = jnp.broadcast_to(best[r], (RS, HD))
                a_ref[t, rows, :] = accum[r]

        return 0

    lax.fori_loop(0, 8, block, 0)


def prepare_kernel(limits, sk_ref, p2, p3, p4, p5, yb, k_out, v_out):
    pages = [p.at[src, 0] for p in (p2, p3, p4, p5) for src in range(2)]
    pages += [yb.at[i] for i in range(8)]
    prepare(limits, HALF, pages, sk_ref, k_out, v_out)


def second_kernel(shift, place, q_ref, k_ref, v_ref, m_ref, a_ref, o_ref):
    t = lax.rem(place[3] + shift, 8)
    live = place[4] - t * ROWS

    @pl.when(live > 0)
    def _():
        q = row_block(q_ref, t)
        parts = RB // RS
        best = [m_ref[t, r * RS:(r + 1) * RS, :][:, :1] for r in range(parts)]
        accum = [a_ref[t, r * RS:(r + 1) * RS, :] for r in range(parts)]
        best, accum = attend(q, k_ref, v_ref, best, accum)
        keep = lax.broadcasted_iota(jnp.int32, (ROWS, HD), 0) < live
        for r in range(parts):
            out = accum[r][:, :HD] / accum[r][:, HD:]
            for h in range(RS // ROWS):
                n = r * (RS // ROWS) + h
                o_ref[:, n * HD:(n + 1) * HD] = jnp.where(keep, out[h * ROWS:(h + 1) * ROWS], 0.0).astype(BF16)

    @pl.when(live <= 0)
    def _():
        o_ref[...] = jnp.zeros(o_ref.shape, BF16)


def gather_kernel(place, *refs):
    out_ref = refs[-1]
    for block, shift in zip(refs, SHIFTS):
        source = lax.rem(place[3] + 8 - shift, 8)
        out_ref[0, :, pl.ds(pl.multiple_of(source * WIDTH, WIDTH), WIDTH)] = block[...]


def holders_of(y, x, c):
    def table(core):
        rows = [(0, 0, 0), (0, 0, 1)]
        rows += [(dy, dx, 0) for dy, dx in TIES]
        rows += [PAIRS[j][core] + (src,) for j in range(EARLY) for src in range(2)]
        rows += [(dy, dx, 1) for dy, dx in TIES]
        rows += [PAIRS[j][1 - core] + (1 - src,) for j in range(EARLY) for src in range(2)]
        rows += [PAIRS[j][core] + (src,) for j in range(EARLY, 6) for src in range(2)]
        rows += [PAIRS[j][1 - core] + (1 - src,) for j in range(EARLY, 6) for src in range(2)]
        return jnp.array(rows, jnp.int32).T

    dy, dx, flip = jnp.where(c == 0, table(0), table(1))
    return ((y - dy) % 4) * 8 + ((x - dx) % 4) * 2 + (c ^ flip)


def chips(first, second):
    pairs = []
    for y in range(4):
        for x in range(4):
            for core, (dy, dx) in ((0, first), (1, second)):
                pairs.append((y * 8 + x * 2 + core, (y + dy) % 4 * 8 + (x + dx) % 4 * 2 + core))
    return pairs


def swap_cores(value):
    return lax.ppermute(value, "cache", [(i, i ^ 1) for i in range(8)])


def local(queries, suffix_keys, suffix_values, prefix_keys, prefix_values, hit_len, suffix_len, page_map):
    y = lax.axis_index("dp").astype(jnp.int32)
    cache = lax.axis_index("cache").astype(jnp.int32)
    x, c = cache // 2, cache % 2
    me = lax.axis_index("tensor").astype(jnp.int32)
    request = y * 8 + cache
    sk, sv = suffix_keys[0], suffix_values[0]
    place = jnp.stack([y, x, c, me, suffix_len[request]])
    holders = holders_of(y, x, c)
    page_index = jnp.sum(
        jnp.where(page_map[request][None, :] == holders[:, None], jnp.arange(32, dtype=jnp.int32)[None, :], 0), axis=1
    )
    limits = hit_len[request] - page_index * PAGE

    page = (2, PAGE, HD)
    n = len(PAIRS)
    shaped = lambda *lead: jax.ShapeDtypeStruct(lead + page, BF16)
    exchange, own_parts, t0, t1, t2, own = pl.pallas_call(
        pack_kernel,
        in_specs=[SMEM, VMEM, VMEM],
        out_specs=[VMEM] * 6,
        out_shape=[shaped(2 * n + 1), shaped(n, 2), shaped(2), shaped(2), shaped(2), shaped()],
        compiler_params=PARAMS,
        name="pack_pages",
        cost_estimate=cost(0, 4 << 20),
    )(place, prefix_keys[0], prefix_values[0])
    exchanged = swap_cores(exchange)
    ties = [lax.ppermute(t, GROUP, chips(d, d)) for t, d in zip((t0, t1, t2), TIES)]
    sends = pl.pallas_call(
        join_kernel,
        in_specs=[VMEM] * 2,
        out_specs=[VMEM] * n,
        out_shape=[shaped(2, 2)] * n,
        compiler_params=PARAMS,
        name="join_pages",
        cost_estimate=cost(0, 4 << 20),
    )(own_parts, exchanged)
    pairs = [lax.ppermute(s, GROUP, chips(*d)) for s, d in zip(sends, PAIRS)]
    ya = swap_cores(jnp.concatenate([t[1:2] for t in ties] + [p[:, 1] for p in pairs[:EARLY]]))
    yb = swap_cores(jnp.concatenate([p[:, 1] for p in pairs[EARLY:]]))

    q = queries[0].reshape(8, ROWS, WIDTH)
    keys = HALF * PAGE
    m, a = pl.pallas_call(
        first_kernel,
        in_specs=[SMEM, SMEM] + [VMEM] * 11,
        out_specs=[VMEM, VMEM],
        out_shape=[jax.ShapeDtypeStruct((8, RB, HD), F32), jax.ShapeDtypeStruct((8, RB, 2 * HD), F32)],
        scratch_shapes=[pltpu.VMEM((keys, HD), BF16), pltpu.VMEM((keys, 2 * HD), BF16)],
        compiler_params=PARAMS,
        name="first_half",
        cost_estimate=cost(4 * 8 * RB * (keys + SUF) * 2 * HD, 16 << 20),
    )(place, limits, q, sk, sv, own, exchanged, *ties, *pairs[:EARLY], ya)
    k2, v2 = pl.pallas_call(
        prepare_kernel,
        in_specs=[SMEM] + [VMEM] * 6,
        out_specs=[VMEM, VMEM],
        out_shape=[jax.ShapeDtypeStruct((keys, HD), BF16), jax.ShapeDtypeStruct((keys, 2 * HD), BF16)],
        compiler_params=PARAMS,
        name="prepare_second",
        cost_estimate=cost(0, 4 << 20),
    )(limits, sk, *pairs[EARLY:], yb)
    blocks = []
    for shift in SHIFTS:
        block = pl.pallas_call(
            functools.partial(second_kernel, shift),
            in_specs=[SMEM] + [VMEM] * 5,
            out_specs=VMEM,
            out_shape=jax.ShapeDtypeStruct((ROWS, WIDTH), BF16),
            compiler_params=PARAMS,
            name="second_half",
            cost_estimate=cost(4 * RB * keys * 2 * HD, 4 << 20),
        )(place, q, k2, v2, m, a)
        if shift:
            block = lax.ppermute(block, "tensor", [(i, (i + shift) % 8) for i in range(8)])
        blocks.append(block)
    return pl.pallas_call(
        gather_kernel,
        in_specs=[SMEM] + [VMEM] * 8,
        out_specs=VMEM,
        out_shape=jax.ShapeDtypeStruct((1, ROWS, 8 * WIDTH), BF16),
        compiler_params=PARAMS,
        name="gather_blocks",
        cost_estimate=cost(0, 4 << 20),
    )(place, *blocks)


def solution(mesh):
    placed = (
        P(GROUP, None, "tensor"),
        P(GROUP, None, "tensor"),
        P(GROUP, None, "tensor"),
        P(GROUP, None, None, "tensor"),
        P(GROUP, None, None, "tensor"),
        P(),
        P(),
        P(),
    )
    return jax.shard_map(
        local, mesh=mesh, in_specs=placed, out_specs=P(GROUP, "tensor", None), check_vma=False
    )
```

```python
import functools
import math

import jax
import jax.numpy as jnp
from jax import lax
from jax.experimental import pallas as pl
from jax.experimental.pallas import tpu as pltpu
from jax.sharding import PartitionSpec as P

HD = 128
HEADS = 16
WIDTH = HEADS * HD
PAGE = 128
PAGES = 32
KEYS = PAGES * PAGE
SUF = 256
ROWS = 32
RB = ROWS * HEADS
TILE = 1024
RS = 512
GROUPS = ((4, 3, 5), (2, 6, 1, 7), (0,))
SCALE = math.log2(math.e) / math.sqrt(HD)
F32 = jnp.float32
BF16 = jnp.bfloat16
DEVICES = ("dp", "cache")
PARAMS = pltpu.CompilerParams(vmem_limit_bytes=24 << 20)
SMEM = pl.BlockSpec(memory_space=pltpu.SMEM)
VMEM = pl.BlockSpec(memory_space=pltpu.VMEM)


def qk(a, b):
    return lax.dot_general(a, b, (((1,), (1,)), ((), ())), preferred_element_type=F32)


def pv(a, b):
    return lax.dot_general(a, b, (((1,), (0,)), ((), ())), preferred_element_type=F32)


def prepare(place, page_map, buf_ref, sk_ref, k_out, v_out):
    first_key = sk_ref[0:1, :].astype(F32)
    slot = lax.broadcasted_iota(jnp.int32, (PAGE, HD), 0)
    request, hit = place[0], place[2]

    def page(p, _):
        holder = page_map[request, p]
        valid = slot < hit - p * PAGE
        rows = pl.ds(pl.multiple_of(p * PAGE, PAGE), PAGE)
        k_out[rows, :] = jnp.where(valid, buf_ref[holder, :PAGE, :].astype(F32), first_key).astype(BF16)
        v_out[rows, :HD] = jnp.where(valid, buf_ref[holder, PAGE:, :].astype(F32), 0.0).astype(BF16)
        v_out[rows, HD:] = jnp.where(valid, 1.0, 0.0).astype(BF16)
        return 0

    lax.fori_loop(0, PAGES, page, 0, unroll=4)


def row_block(q_ref, t):
    q = jnp.concatenate([q_ref[t, :, n * HD:(n + 1) * HD] for n in range(HEADS)], axis=0)
    scaled = q.astype(F32) * SCALE
    high = scaled.astype(BF16)
    low = (scaled - high.astype(F32)).astype(BF16)
    return jnp.concatenate([high, low], axis=1)


def attend(t, live, q_ref, sk_ref, sv_ref, k_ref, v_ref, o_ref):
    q = row_block(q_ref, t)
    slot = t * ROWS + lax.broadcasted_iota(jnp.int32, (RS, SUF), 0) % ROWS
    causal = lax.broadcasted_iota(jnp.int32, (RS, SUF), 1) <= slot
    parts = RB // RS
    units = [(r, j) for j in range(-1, KEYS // TILE) for r in range(parts)]

    def keys(j):
        return sk_ref[...] if j < 0 else k_ref[j * TILE:(j + 1) * TILE, :]

    def values(j):
        if j < 0:
            return jnp.concatenate([sv_ref[...], jnp.ones((SUF, HD), BF16)], axis=1)
        return v_ref[j * TILE:(j + 1) * TILE, :]

    def score(unit):
        r, j = unit
        s = qk(q[r * RS:(r + 1) * RS], jnp.concatenate([keys(j)] * 2, axis=1))
        return jnp.where(causal, s, -jnp.inf) if j < 0 else s

    best, accum = [None] * parts, [None] * parts
    ahead = score(units[0])
    for i, (r, j) in enumerate(units):
        s = ahead
        if i + 1 < len(units):
            ahead = score(units[i + 1])
        top = jnp.max(s, axis=1, keepdims=True)
        if j < 0:
            best[r] = top
            accum[r] = pv(jnp.exp2(s - top).astype(BF16), values(j))
        else:
            new = jnp.maximum(best[r], top)
            p = jnp.exp2(s - new).astype(BF16)
            accum[r] = accum[r] * jnp.exp2(best[r] - new) + pv(p, values(j))
            best[r] = new
    keep = lax.broadcasted_iota(jnp.int32, (ROWS, HD), 0) < live
    for r in range(parts):
        out = accum[r][:, :HD] / accum[r][:, HD:]
        for h in range(RS // ROWS):
            n = r * (RS // ROWS) + h
            o_ref[:, n * HD:(n + 1) * HD] = jnp.where(keep, out[h * ROWS:(h + 1) * ROWS], 0.0).astype(BF16)


def attend_group(shifts, place, q_ref, sk_ref, sv_ref, k_ref, v_ref, out_refs):
    for shift, o_ref in zip(shifts, out_refs):
        t = lax.rem(place[1] + shift, 8)
        attend(t, place[3] - t * ROWS, q_ref, sk_ref, sv_ref, k_ref, v_ref, o_ref)


def first_kernel(shifts, place, page_map, q_ref, sk_ref, sv_ref, buf_ref, k_ref, v_ref, *out_refs):
    prepare(place, page_map, buf_ref, sk_ref, k_ref, v_ref)
    attend_group(shifts, place, q_ref, sk_ref, sv_ref, k_ref, v_ref, out_refs)


def later_kernel(shifts, place, q_ref, sk_ref, sv_ref, k_ref, v_ref, *refs):
    attend_group(shifts, place, q_ref, sk_ref, sv_ref, k_ref, v_ref, refs[-len(shifts):])


def gather_kernel(place, *refs):
    out_ref = refs[-1]
    for block, shift in zip(refs, sum(GROUPS, ())):
        source = lax.rem(place[1] + 8 - shift, 8)
        out_ref[0, :, pl.ds(pl.multiple_of(source * WIDTH, WIDTH), WIDTH)] = block[...]


def local(queries, suffix_keys, suffix_values, prefix_keys, prefix_values, hit_len, suffix_len, page_map):
    request = lax.axis_index(DEVICES).astype(jnp.int32)
    me = lax.axis_index("tensor").astype(jnp.int32)
    q = queries[0].reshape(8, ROWS, WIDTH)
    sk, sv = suffix_keys[0], suffix_values[0]
    packed = jnp.concatenate([prefix_keys[0], prefix_values[0]], axis=1)
    buf = lax.all_to_all(packed, DEVICES, split_axis=0, concat_axis=0, tiled=True)
    place = jnp.stack([request, me, hit_len[request], suffix_len[request]])
    block = jax.ShapeDtypeStruct((ROWS, WIDTH), BF16)
    keys = [jax.ShapeDtypeStruct((KEYS, HD), BF16), jax.ShapeDtypeStruct((KEYS, 2 * HD), BF16)]
    k, v, *blocks = pl.pallas_call(
        functools.partial(first_kernel, GROUPS[0]),
        in_specs=[SMEM, SMEM] + [VMEM] * 4,
        out_specs=[VMEM] * (2 + len(GROUPS[0])),
        out_shape=keys + [block] * len(GROUPS[0]),
        compiler_params=PARAMS,
        name="attend_first",
    )(place, page_map, q, sk, sv, buf)
    def send(blocks, shifts):
        return [
            lax.ppermute(x, "tensor", [(z, (z + d) % 8) for z in range(8)]) if d else x
            for x, d in zip(blocks, shifts)
        ]

    sent = [send(blocks, GROUPS[0])]
    for i, shifts in enumerate(GROUPS[1:]):
        arrived = sent[i - 1] if i else []
        blocks = pl.pallas_call(
            functools.partial(later_kernel, shifts),
            in_specs=[SMEM] + [VMEM] * 5 + [pl.BlockSpec(memory_space=pl.ANY)] * len(arrived),
            out_specs=[VMEM] * len(shifts),
            out_shape=[block] * len(shifts),
            compiler_params=PARAMS,
            name="attend_later",
        )(place, q, sk, sv, k, v, *arrived)
        sent.append(send(blocks, shifts))
    blocks = sum(sent, [])
    return pl.pallas_call(
        gather_kernel,
        in_specs=[SMEM] + [VMEM] * 8,
        out_specs=VMEM,
        out_shape=jax.ShapeDtypeStruct((1, ROWS, 8 * WIDTH), BF16),
        compiler_params=PARAMS,
        name="gather_blocks",
    )(place, *blocks)


def solution(mesh):
    placed = (
        P(DEVICES, None, "tensor"),
        P(DEVICES, None, "tensor"),
        P(DEVICES, None, "tensor"),
        P(DEVICES, None, None, "tensor"),
        P(DEVICES, None, None, "tensor"),
        P(),
        P(),
        P(),
    )
    return jax.shard_map(
        local, mesh=mesh, in_specs=placed, out_specs=P(DEVICES, "tensor", None), check_vma=False
    )
```

```python
import functools
import math

import jax
import jax.numpy as jnp
from jax import lax
from jax.experimental import pallas as pl
from jax.experimental.pallas import tpu as pltpu
from jax.sharding import PartitionSpec as P

HD = 128
HEADS = 16
WIDTH = HEADS * HD
PAGE = 128
PAGES = 32
KEYS = PAGES * PAGE
SUF = 256
ROWS = 32
RB = ROWS * HEADS
TILE = 1024
RS = 512
GROUPS = ((4, 5, 3), (6, 2, 7, 1), (0,))
SCALE = math.log2(math.e) / math.sqrt(HD)
F32 = jnp.float32
BF16 = jnp.bfloat16
DEVICES = ("dp", "cache")
PARAMS = pltpu.CompilerParams(vmem_limit_bytes=24 << 20)
SMEM = pl.BlockSpec(memory_space=pltpu.SMEM)
VMEM = pl.BlockSpec(memory_space=pltpu.VMEM)


def qk(a, b):
    return lax.dot_general(a, b, (((1,), (1,)), ((), ())), preferred_element_type=F32)


def pv(a, b):
    return lax.dot_general(a, b, (((1,), (0,)), ((), ())), preferred_element_type=F32)


def prepare(place, page_map, buf_ref, sk_ref, k_out, v_out):
    request, hit = place[0], place[2]

    def page(p, whole):
        holder = page_map[request, p]
        rows = pl.ds(pl.multiple_of(p * PAGE, PAGE), PAGE)
        if whole:
            k_out[rows, :] = buf_ref[holder, :PAGE, :]
            v_out[rows, :HD] = buf_ref[holder, PAGE:, :]
            v_out[rows, HD:] = jnp.ones((PAGE, HD), BF16)
        else:
            valid = lax.broadcasted_iota(jnp.int32, (PAGE, HD), 0) < hit - p * PAGE
            k, v = buf_ref[holder, :PAGE, :].astype(F32), buf_ref[holder, PAGE:, :].astype(F32)
            k_out[rows, :] = jnp.where(valid, k, sk_ref[0:1, :].astype(F32)).astype(BF16)
            v_out[rows, :HD] = jnp.where(valid, v, 0.0).astype(BF16)
            v_out[rows, HD:] = jnp.where(valid, 1.0, 0.0).astype(BF16)

    def tile(j, _):
        for whole in (True, False):
            @pl.when((hit >= (j + 1) * TILE) == whole)
            def _(whole=whole):
                for i in range(TILE // PAGE):
                    page(j * (TILE // PAGE) + i, whole)

        return 0

    lax.fori_loop(0, KEYS // TILE, tile, 0)


def row_block(q_ref, t):
    q = jnp.concatenate([q_ref[t, :, n * HD:(n + 1) * HD] for n in range(HEADS)], axis=0)
    scaled = q.astype(F32) * SCALE
    high = scaled.astype(BF16)
    low = (scaled - high.astype(F32)).astype(BF16)
    return jnp.concatenate([high, low], axis=1)


def attend(t, live, q_ref, sk_ref, sv_ref, k_ref, v_ref, o_ref):
    q = row_block(q_ref, t)
    slot = t * ROWS + lax.broadcasted_iota(jnp.int32, (RS, SUF), 0) % ROWS
    causal = lax.broadcasted_iota(jnp.int32, (RS, SUF), 1) <= slot
    parts = RB // RS
    units = [(r, j) for j in range(-1, KEYS // TILE) for r in range(parts)]

    def keys(j):
        return sk_ref[...] if j < 0 else k_ref[j * TILE:(j + 1) * TILE, :]

    def values(j):
        if j < 0:
            return jnp.concatenate([sv_ref[...], jnp.ones((SUF, HD), BF16)], axis=1)
        return v_ref[j * TILE:(j + 1) * TILE, :]

    def score(unit):
        r, j = unit
        s = qk(q[r * RS:(r + 1) * RS], jnp.concatenate([keys(j)] * 2, axis=1))
        return jnp.where(causal, s, -jnp.inf) if j < 0 else s

    best, accum = [None] * parts, [None] * parts
    ahead = score(units[0])
    for i, (r, j) in enumerate(units):
        s = ahead
        if i + 1 < len(units):
            ahead = score(units[i + 1])
        top = jnp.max(s, axis=1, keepdims=True)
        if j < 0:
            best[r] = top
            accum[r] = pv(jnp.exp2(s - top).astype(BF16), values(j))
        else:
            new = jnp.maximum(best[r], top)
            p = jnp.exp2(s - new).astype(BF16)
            accum[r] = accum[r] * jnp.exp2(best[r] - new) + pv(p, values(j))
            best[r] = new
    keep = lax.broadcasted_iota(jnp.int32, (ROWS, HD), 0) < live
    for r in range(parts):
        out = accum[r][:, :HD] / accum[r][:, HD:]
        for h in range(RS // ROWS):
            n = r * (RS // ROWS) + h
            o_ref[:, n * HD:(n + 1) * HD] = jnp.where(keep, out[h * ROWS:(h + 1) * ROWS], 0.0).astype(BF16)


def attend_group(shifts, place, q_ref, sk_ref, sv_ref, k_ref, v_ref, out_refs):
    for shift, o_ref in zip(shifts, out_refs):
        t = lax.rem(place[1] + shift, 8)
        attend(t, place[3] - t * ROWS, q_ref, sk_ref, sv_ref, k_ref, v_ref, o_ref)


def first_kernel(shifts, place, page_map, q_ref, sk_ref, sv_ref, buf_ref, k_ref, v_ref, *out_refs):
    prepare(place, page_map, buf_ref, sk_ref, k_ref, v_ref)
    attend_group(shifts, place, q_ref, sk_ref, sv_ref, k_ref, v_ref, out_refs)


def later_kernel(shifts, place, q_ref, sk_ref, sv_ref, k_ref, v_ref, *refs):
    attend_group(shifts, place, q_ref, sk_ref, sv_ref, k_ref, v_ref, refs[-len(shifts):])


def gather_kernel(place, *refs):
    out_ref = refs[-1]
    for block, shift in zip(refs, sum(GROUPS, ())):
        source = lax.rem(place[1] + 8 - shift, 8)
        out_ref[0, :, pl.ds(pl.multiple_of(source * WIDTH, WIDTH), WIDTH)] = block[...]


def local(queries, suffix_keys, suffix_values, prefix_keys, prefix_values, hit_len, suffix_len, page_map):
    request = lax.axis_index(DEVICES).astype(jnp.int32)
    me = lax.axis_index("tensor").astype(jnp.int32)
    q = queries[0].reshape(8, ROWS, WIDTH)
    sk, sv = suffix_keys[0], suffix_values[0]
    packed = jnp.concatenate([prefix_keys[0], prefix_values[0]], axis=1)
    buf = lax.all_to_all(packed, DEVICES, split_axis=0, concat_axis=0, tiled=True)
    place = jnp.stack([request, me, hit_len[request], suffix_len[request]])
    block = jax.ShapeDtypeStruct((ROWS, WIDTH), BF16)
    keys = [jax.ShapeDtypeStruct((KEYS, HD), BF16), jax.ShapeDtypeStruct((KEYS, 2 * HD), BF16)]
    k, v, *blocks = pl.pallas_call(
        functools.partial(first_kernel, GROUPS[0]),
        in_specs=[SMEM, SMEM] + [VMEM] * 4,
        out_specs=[VMEM] * (2 + len(GROUPS[0])),
        out_shape=keys + [block] * len(GROUPS[0]),
        compiler_params=PARAMS,
        name="attend_first",
    )(place, page_map, q, sk, sv, buf)
    def send(blocks, shifts):
        return [
            lax.ppermute(x, "tensor", [(z, (z + d) % 8) for z in range(8)]) if d else x
            for x, d in zip(blocks, shifts)
        ]

    sent = [send(blocks, GROUPS[0])]
    for i, shifts in enumerate(GROUPS[1:]):
        arrived = sent[i - 1] if i else []
        blocks = pl.pallas_call(
            functools.partial(later_kernel, shifts),
            in_specs=[SMEM] + [VMEM] * 5 + [pl.BlockSpec(memory_space=pl.ANY)] * len(arrived),
            out_specs=[VMEM] * len(shifts),
            out_shape=[block] * len(shifts),
            compiler_params=PARAMS,
            name="attend_later",
        )(place, q, sk, sv, k, v, *arrived)
        sent.append(send(blocks, shifts))
    blocks = sum(sent, [])
    return pl.pallas_call(
        gather_kernel,
        in_specs=[SMEM] + [VMEM] * 8,
        out_specs=VMEM,
        out_shape=jax.ShapeDtypeStruct((1, ROWS, 8 * WIDTH), BF16),
        compiler_params=PARAMS,
        name="gather_blocks",
    )(place, *blocks)


def solution(mesh):
    placed = (
        P(DEVICES, None, "tensor"),
        P(DEVICES, None, "tensor"),
        P(DEVICES, None, "tensor"),
        P(DEVICES, None, None, "tensor"),
        P(DEVICES, None, None, "tensor"),
        P(),
        P(),
        P(),
    )
    return jax.shard_map(
        local, mesh=mesh, in_specs=placed, out_specs=P(DEVICES, "tensor", None), check_vma=False
    )
```

```python
import functools
import math

import jax
import jax.numpy as jnp
from jax import lax
from jax.experimental import pallas as pl
from jax.experimental.pallas import tpu as pltpu
from jax.sharding import PartitionSpec as P

HD = 128
HEADS = 16
WIDTH = HEADS * HD
PAGE = 128
PAGES = 32
KEYS = PAGES * PAGE
SUF = 256
ROWS = 32
RB = ROWS * HEADS
TILE = 1024
RS = 512
GROUPS = ((4, 5), (3, 6, 2), (7, 1), (0,))
SCALE = math.log2(math.e) / math.sqrt(HD)
F32 = jnp.float32
BF16 = jnp.bfloat16
DEVICES = ("dp", "cache")
PARAMS = pltpu.CompilerParams(vmem_limit_bytes=24 << 20)
SMEM = pl.BlockSpec(memory_space=pltpu.SMEM)
VMEM = pl.BlockSpec(memory_space=pltpu.VMEM)


def qk(a, b):
    return lax.dot_general(a, b, (((1,), (1,)), ((), ())), preferred_element_type=F32)


def pv(a, b):
    return lax.dot_general(a, b, (((1,), (0,)), ((), ())), preferred_element_type=F32)


def prepare(place, page_map, buf_ref, sk_ref, k_out, v_out):
    request, hit = place[0], place[2]

    def page(p, whole):
        holder = page_map[request, p]
        rows = pl.ds(pl.multiple_of(p * PAGE, PAGE), PAGE)
        if whole:
            k_out[rows, :] = buf_ref[holder, :PAGE, :]
            v_out[rows, :HD] = buf_ref[holder, PAGE:, :]
            v_out[rows, HD:] = jnp.ones((PAGE, HD), BF16)
        else:
            valid = lax.broadcasted_iota(jnp.int32, (PAGE, HD), 0) < hit - p * PAGE
            k, v = buf_ref[holder, :PAGE, :].astype(F32), buf_ref[holder, PAGE:, :].astype(F32)
            k_out[rows, :] = jnp.where(valid, k, sk_ref[0:1, :].astype(F32)).astype(BF16)
            v_out[rows, :HD] = jnp.where(valid, v, 0.0).astype(BF16)
            v_out[rows, HD:] = jnp.where(valid, 1.0, 0.0).astype(BF16)

    def tile(j, _):
        for whole in (True, False):
            @pl.when((hit >= (j + 1) * TILE) == whole)
            def _(whole=whole):
                for i in range(TILE // PAGE):
                    page(j * (TILE // PAGE) + i, whole)

        return 0

    lax.fori_loop(0, KEYS // TILE, tile, 0)


def row_block(q_ref, t):
    q = jnp.concatenate([q_ref[t, :, n * HD:(n + 1) * HD] for n in range(HEADS)], axis=0)
    scaled = q.astype(F32) * SCALE
    high = scaled.astype(BF16)
    low = (scaled - high.astype(F32)).astype(BF16)
    return jnp.concatenate([high, low], axis=1)


def attend(t, live, q_ref, sk_ref, sv_ref, k_ref, v_ref, o_ref):
    q = row_block(q_ref, t)
    slot = t * ROWS + lax.broadcasted_iota(jnp.int32, (RS, SUF), 0) % ROWS
    causal = lax.broadcasted_iota(jnp.int32, (RS, SUF), 1) <= slot
    parts = RB // RS
    units = [(r, j) for j in range(-1, KEYS // TILE) for r in range(parts)]

    def keys(j):
        return sk_ref[...] if j < 0 else k_ref[j * TILE:(j + 1) * TILE, :]

    def values(j):
        if j < 0:
            return jnp.concatenate([sv_ref[...], jnp.ones((SUF, HD), BF16)], axis=1)
        return v_ref[j * TILE:(j + 1) * TILE, :]

    def score(unit):
        r, j = unit
        s = qk(q[r * RS:(r + 1) * RS], jnp.concatenate([keys(j)] * 2, axis=1))
        return jnp.where(causal, s, -jnp.inf) if j < 0 else s

    best, accum = [None] * parts, [None] * parts
    ahead = score(units[0])
    for i, (r, j) in enumerate(units):
        s = ahead
        if i + 1 < len(units):
            ahead = score(units[i + 1])
        top = jnp.max(s, axis=1, keepdims=True)
        if j < 0:
            best[r] = top
            accum[r] = pv(jnp.exp2(s - top).astype(BF16), values(j))
        else:
            new = jnp.maximum(best[r], top)
            p = jnp.exp2(s - new).astype(BF16)
            accum[r] = accum[r] * jnp.exp2(best[r] - new) + pv(p, values(j))
            best[r] = new
    keep = lax.broadcasted_iota(jnp.int32, (ROWS, HD), 0) < live
    for r in range(parts):
        out = accum[r][:, :HD] / accum[r][:, HD:]
        for h in range(RS // ROWS):
            n = r * (RS // ROWS) + h
            o_ref[:, n * HD:(n + 1) * HD] = jnp.where(keep, out[h * ROWS:(h + 1) * ROWS], 0.0).astype(BF16)


def attend_group(shifts, place, q_ref, sk_ref, sv_ref, k_ref, v_ref, out_refs):
    for shift, o_ref in zip(shifts, out_refs):
        t = lax.rem(place[1] + shift, 8)
        attend(t, place[3] - t * ROWS, q_ref, sk_ref, sv_ref, k_ref, v_ref, o_ref)


def first_kernel(shifts, hit_len, suffix_len, page_map, q_ref, sk_ref, sv_ref, buf_ref, place, k_ref, v_ref, *out_refs):
    request = lax.axis_index("dp") * 8 + lax.axis_index("cache")
    place[0] = request
    place[1] = lax.axis_index("tensor")
    place[2] = hit_len[request]
    place[3] = suffix_len[request]
    prepare(place, page_map, buf_ref, sk_ref, k_ref, v_ref)
    attend_group(shifts, place, q_ref, sk_ref, sv_ref, k_ref, v_ref, out_refs)


def later_kernel(shifts, place, q_ref, sk_ref, sv_ref, k_ref, v_ref, *refs):
    attend_group(shifts, place, q_ref, sk_ref, sv_ref, k_ref, v_ref, refs[-len(shifts):])


def gather_kernel(place, *refs):
    out_ref = refs[-1]
    for block, shift in zip(refs, sum(GROUPS, ())):
        source = lax.rem(place[1] + 8 - shift, 8)
        out_ref[0, :, pl.ds(pl.multiple_of(source * WIDTH, WIDTH), WIDTH)] = block[...]


def local(queries, suffix_keys, suffix_values, prefix_keys, prefix_values, hit_len, suffix_len, page_map):
    q = queries[0].reshape(8, ROWS, WIDTH)
    sk, sv = suffix_keys[0], suffix_values[0]
    packed = jnp.concatenate([prefix_keys[0], prefix_values[0]], axis=1)
    buf = lax.all_to_all(packed, DEVICES, split_axis=0, concat_axis=0, tiled=True)
    block = jax.ShapeDtypeStruct((ROWS, WIDTH), BF16)
    keys = [jax.ShapeDtypeStruct((KEYS, HD), BF16), jax.ShapeDtypeStruct((KEYS, 2 * HD), BF16)]
    place, k, v, *blocks = pl.pallas_call(
        functools.partial(first_kernel, GROUPS[0]),
        in_specs=[SMEM] * 3 + [VMEM] * 4,
        out_specs=[SMEM] + [VMEM] * (2 + len(GROUPS[0])),
        out_shape=[jax.ShapeDtypeStruct((4,), jnp.int32)] + keys + [block] * len(GROUPS[0]),
        compiler_params=PARAMS,
        name="attend_first",
    )(hit_len, suffix_len, page_map, q, sk, sv, buf)
    def send(blocks, shifts):
        return [
            lax.ppermute(x, "tensor", [(z, (z + d) % 8) for z in range(8)]) if d else x
            for x, d in zip(blocks, shifts)
        ]

    sent = [send(blocks, GROUPS[0])]
    for i, shifts in enumerate(GROUPS[1:]):
        arrived = sent[i - 1] if i else []
        if i == len(GROUPS) - 2:
            arrived = arrived[:1]
        blocks = pl.pallas_call(
            functools.partial(later_kernel, shifts),
            in_specs=[SMEM] + [VMEM] * 5 + [pl.BlockSpec(memory_space=pl.ANY)] * len(arrived),
            out_specs=[VMEM] * len(shifts),
            out_shape=[block] * len(shifts),
            compiler_params=PARAMS,
            name="attend_later",
        )(place, q, sk, sv, k, v, *arrived)
        sent.append(send(blocks, shifts))
    blocks = sum(sent, [])
    return pl.pallas_call(
        gather_kernel,
        in_specs=[SMEM] + [VMEM] * 8,
        out_specs=VMEM,
        out_shape=jax.ShapeDtypeStruct((1, ROWS, 8 * WIDTH), BF16),
        compiler_params=PARAMS,
        name="gather_blocks",
    )(place, *blocks)


def solution(mesh):
    placed = (
        P(DEVICES, None, "tensor"),
        P(DEVICES, None, "tensor"),
        P(DEVICES, None, "tensor"),
        P(DEVICES, None, None, "tensor"),
        P(DEVICES, None, None, "tensor"),
        P(),
        P(),
        P(),
    )
    return jax.shard_map(
        local, mesh=mesh, in_specs=placed, out_specs=P(DEVICES, "tensor", None), check_vma=False
    )
```

```python
import functools
import math

import jax
import jax.numpy as jnp
from jax import lax
from jax.experimental import pallas as pl
from jax.experimental.pallas import tpu as pltpu
from jax.sharding import PartitionSpec as P

HD = 128
HEADS = 16
WIDTH = HEADS * HD
PAGE = 128
PAGES = 32
KEYS = PAGES * PAGE
SUF = 256
ROWS = 32
RB = ROWS * HEADS
TILE = 1024
RS = 512
GROUPS = ((3, 5), (4, 6, 2), (7, 1), (0,))
SCALE = math.log2(math.e) / math.sqrt(HD)
F32 = jnp.float32
BF16 = jnp.bfloat16
DEVICES = ("dp", "cache")
PARAMS = pltpu.CompilerParams(vmem_limit_bytes=24 << 20)
SMEM = pl.BlockSpec(memory_space=pltpu.SMEM)
VMEM = pl.BlockSpec(memory_space=pltpu.VMEM)


def qk(a, b):
    return lax.dot_general(a, b, (((1,), (1,)), ((), ())), preferred_element_type=F32)


def pv(a, b):
    return lax.dot_general(a, b, (((1,), (0,)), ((), ())), preferred_element_type=F32)


def prepare(place, page_map, buf_ref, sk_ref, k_out, v_out):
    request, hit = place[0], place[2]

    def page(p, whole):
        holder = page_map[request, p]
        rows = pl.ds(pl.multiple_of(p * PAGE, PAGE), PAGE)
        if whole:
            k_out[rows, :] = buf_ref[holder, :PAGE, :]
            v_out[rows, :HD] = buf_ref[holder, PAGE:, :]
            v_out[rows, HD:] = jnp.ones((PAGE, HD), BF16)
        else:
            valid = lax.broadcasted_iota(jnp.int32, (PAGE, HD), 0) < hit - p * PAGE
            k, v = buf_ref[holder, :PAGE, :].astype(F32), buf_ref[holder, PAGE:, :].astype(F32)
            k_out[rows, :] = jnp.where(valid, k, sk_ref[0:1, :].astype(F32)).astype(BF16)
            v_out[rows, :HD] = jnp.where(valid, v, 0.0).astype(BF16)
            v_out[rows, HD:] = jnp.where(valid, 1.0, 0.0).astype(BF16)

    def tile(j, _):
        for whole in (True, False):
            @pl.when((hit >= (j + 1) * TILE) == whole)
            def _(whole=whole):
                for i in range(TILE // PAGE):
                    page(j * (TILE // PAGE) + i, whole)

        return 0

    lax.fori_loop(0, KEYS // TILE, tile, 0)


def row_block(q_ref, t):
    q = jnp.concatenate([q_ref[t, :, n * HD:(n + 1) * HD] for n in range(HEADS)], axis=0)
    scaled = q.astype(F32) * SCALE
    high = scaled.astype(BF16)
    low = (scaled - high.astype(F32)).astype(BF16)
    return jnp.concatenate([high, low], axis=1)


def attend(t, live, q_ref, sk_ref, sv_ref, k_ref, v_ref, o_ref):
    q = row_block(q_ref, t)
    slot = t * ROWS + lax.broadcasted_iota(jnp.int32, (RS, SUF), 0) % ROWS
    causal = lax.broadcasted_iota(jnp.int32, (RS, SUF), 1) <= slot
    parts = RB // RS
    units = [(r, j) for j in range(-1, KEYS // TILE) for r in range(parts)]

    def keys(j):
        return sk_ref[...] if j < 0 else k_ref[j * TILE:(j + 1) * TILE, :]

    def values(j):
        if j < 0:
            return jnp.concatenate([sv_ref[...], jnp.ones((SUF, HD), BF16)], axis=1)
        return v_ref[j * TILE:(j + 1) * TILE, :]

    def score(unit):
        r, j = unit
        s = qk(q[r * RS:(r + 1) * RS], jnp.concatenate([keys(j)] * 2, axis=1))
        return jnp.where(causal, s, -jnp.inf) if j < 0 else s

    best, accum = [None] * parts, [None] * parts
    ahead = score(units[0])
    for i, (r, j) in enumerate(units):
        s = ahead
        if i + 1 < len(units):
            ahead = score(units[i + 1])
        top = jnp.max(s, axis=1, keepdims=True)
        if j < 0:
            best[r] = top
            accum[r] = pv(jnp.exp2(s - top).astype(BF16), values(j))
        else:
            new = jnp.maximum(best[r], top)
            p = jnp.exp2(s - new).astype(BF16)
            accum[r] = accum[r] * jnp.exp2(best[r] - new) + pv(p, values(j))
            best[r] = new
    keep = lax.broadcasted_iota(jnp.int32, (ROWS, HD), 0) < live
    for r in range(parts):
        out = accum[r][:, :HD] / accum[r][:, HD:]
        for h in range(RS // ROWS):
            n = r * (RS // ROWS) + h
            o_ref[:, n * HD:(n + 1) * HD] = jnp.where(keep, out[h * ROWS:(h + 1) * ROWS], 0.0).astype(BF16)


def attend_group(shifts, place, q_ref, sk_ref, sv_ref, k_ref, v_ref, out_refs):
    for shift, o_ref in zip(shifts, out_refs):
        t = lax.rem(place[1] + shift, 8)
        attend(t, place[3] - t * ROWS, q_ref, sk_ref, sv_ref, k_ref, v_ref, o_ref)


def first_kernel(shifts, hit_len, suffix_len, page_map, q_ref, sk_ref, sv_ref, buf_ref, place, k_ref, v_ref, *out_refs):
    request = lax.axis_index("dp") * 8 + lax.axis_index("cache")
    place[0] = request
    place[1] = lax.axis_index("tensor")
    place[2] = hit_len[request]
    place[3] = suffix_len[request]
    prepare(place, page_map, buf_ref, sk_ref, k_ref, v_ref)
    attend_group(shifts, place, q_ref, sk_ref, sv_ref, k_ref, v_ref, out_refs)


def later_kernel(shifts, place, q_ref, sk_ref, sv_ref, k_ref, v_ref, *refs):
    attend_group(shifts, place, q_ref, sk_ref, sv_ref, k_ref, v_ref, refs[-len(shifts):])


def gather_kernel(place, *refs):
    out_ref = refs[-1]
    for block, shift in zip(refs, sum(GROUPS, ())):
        source = lax.rem(place[1] + 8 - shift, 8)
        out_ref[0, :, pl.ds(pl.multiple_of(source * WIDTH, WIDTH), WIDTH)] = block[...]


def local(queries, suffix_keys, suffix_values, prefix_keys, prefix_values, hit_len, suffix_len, page_map):
    q = queries[0].reshape(8, ROWS, WIDTH)
    sk, sv = suffix_keys[0], suffix_values[0]
    packed = jnp.concatenate([prefix_keys[0], prefix_values[0]], axis=1)
    buf = lax.all_to_all(packed, DEVICES, split_axis=0, concat_axis=0, tiled=True)
    block = jax.ShapeDtypeStruct((ROWS, WIDTH), BF16)
    keys = [jax.ShapeDtypeStruct((KEYS, HD), BF16), jax.ShapeDtypeStruct((KEYS, 2 * HD), BF16)]
    place, k, v, *blocks = pl.pallas_call(
        functools.partial(first_kernel, GROUPS[0]),
        in_specs=[SMEM] * 3 + [VMEM] * 4,
        out_specs=[SMEM] + [VMEM] * (2 + len(GROUPS[0])),
        out_shape=[jax.ShapeDtypeStruct((4,), jnp.int32)] + keys + [block] * len(GROUPS[0]),
        compiler_params=PARAMS,
        name="attend_first",
    )(hit_len, suffix_len, page_map, q, sk, sv, buf)
    def send(blocks, shifts):
        return [
            lax.ppermute(x, "tensor", [(z, (z + d) % 8) for z in range(8)]) if d else x
            for x, d in zip(blocks, shifts)
        ]

    sent = [send(blocks, GROUPS[0])]
    for i, shifts in enumerate(GROUPS[1:]):
        arrived = sent[i - 1] if i else []
        if i == len(GROUPS) - 2:
            arrived = arrived[:1]
        blocks = pl.pallas_call(
            functools.partial(later_kernel, shifts),
            in_specs=[SMEM] + [VMEM] * 5 + [pl.BlockSpec(memory_space=pl.ANY)] * len(arrived),
            out_specs=[VMEM] * len(shifts),
            out_shape=[block] * len(shifts),
            compiler_params=PARAMS,
            name="attend_later",
        )(place, q, sk, sv, k, v, *arrived)
        sent.append(send(blocks, shifts))
    blocks = sum(sent, [])
    return pl.pallas_call(
        gather_kernel,
        in_specs=[SMEM] + [VMEM] * 8,
        out_specs=VMEM,
        out_shape=jax.ShapeDtypeStruct((1, ROWS, 8 * WIDTH), BF16),
        compiler_params=PARAMS,
        name="gather_blocks",
    )(place, *blocks)


def solution(mesh):
    placed = (
        P(DEVICES, None, "tensor"),
        P(DEVICES, None, "tensor"),
        P(DEVICES, None, "tensor"),
        P(DEVICES, None, None, "tensor"),
        P(DEVICES, None, None, "tensor"),
        P(),
        P(),
        P(),
    )
    return jax.shard_map(
        local, mesh=mesh, in_specs=placed, out_specs=P(DEVICES, "tensor", None), check_vma=False
    )
```

```python
import functools
import math

import jax
import jax.numpy as jnp
from jax import lax
from jax.experimental import pallas as pl
from jax.experimental.pallas import tpu as pltpu
from jax.sharding import PartitionSpec as P

HD = 128
HEADS = 16
WIDTH = HEADS * HD
PAGE = 128
PAGES = 32
KEYS = PAGES * PAGE
SUF = 256
ROWS = 32
RB = ROWS * HEADS
TILE = 1024
RS = 512
GROUPS = ((3, 5), (4, 6, 2), (7, 1), (0,))
SCALE = math.log2(math.e) / math.sqrt(HD)
F32 = jnp.float32
BF16 = jnp.bfloat16
DEVICES = ("dp", "cache")
PARAMS = pltpu.CompilerParams(vmem_limit_bytes=24 << 20)
SMEM = pl.BlockSpec(memory_space=pltpu.SMEM)
VMEM = pl.BlockSpec(memory_space=pltpu.VMEM)


def qk(a, b):
    return lax.dot_general(a, b, (((1,), (1,)), ((), ())), preferred_element_type=F32)


def pv(a, b):
    return lax.dot_general(a, b, (((1,), (0,)), ((), ())), preferred_element_type=F32)


def prepare(place, page_map, buf_ref, sk_ref, k_out, v_out):
    request, hit = place[0], place[2]

    def page(p, whole):
        holder = page_map[request, p]
        rows = pl.ds(pl.multiple_of(p * PAGE, PAGE), PAGE)
        if whole:
            k_out[rows, :] = buf_ref[holder, :PAGE, :]
            v_out[rows, :HD] = buf_ref[holder, PAGE:, :]
            v_out[rows, HD:] = jnp.ones((PAGE, HD), BF16)
        else:
            valid = lax.broadcasted_iota(jnp.int32, (PAGE, HD), 0) < hit - p * PAGE
            k, v = buf_ref[holder, :PAGE, :].astype(F32), buf_ref[holder, PAGE:, :].astype(F32)
            k_out[rows, :] = jnp.where(valid, k, sk_ref[0:1, :].astype(F32)).astype(BF16)
            v_out[rows, :HD] = jnp.where(valid, v, 0.0).astype(BF16)
            v_out[rows, HD:] = jnp.where(valid, 1.0, 0.0).astype(BF16)

    def tile(j, _):
        for whole in (True, False):
            @pl.when((hit >= (j + 1) * TILE) == whole)
            def _(whole=whole):
                for i in range(TILE // PAGE):
                    page(j * (TILE // PAGE) + i, whole)

        return 0

    lax.fori_loop(0, KEYS // TILE, tile, 0)


def row_block(q_ref, t):
    q = jnp.concatenate([q_ref[t, :, n * HD:(n + 1) * HD] for n in range(HEADS)], axis=0)
    scaled = q.astype(F32) * SCALE
    high = scaled.astype(BF16)
    low = (scaled - high.astype(F32)).astype(BF16)
    return jnp.concatenate([high, low], axis=1)


def attend(t, live, q_ref, sk_ref, sv_ref, k_ref, v_ref, o_ref):
    q = row_block(q_ref, t)
    slot = t * ROWS + lax.broadcasted_iota(jnp.int32, (RS, SUF), 0) % ROWS
    causal = lax.broadcasted_iota(jnp.int32, (RS, SUF), 1) <= slot
    parts = RB // RS
    units = [(r, j) for j in range(-1, KEYS // TILE) for r in range(parts)]

    def keys(j):
        return sk_ref[...] if j < 0 else k_ref[j * TILE:(j + 1) * TILE, :]

    def values(j):
        if j < 0:
            return jnp.concatenate([sv_ref[...], jnp.ones((SUF, HD), BF16)], axis=1)
        return v_ref[j * TILE:(j + 1) * TILE, :]

    def score(unit):
        r, j = unit
        s = qk(q[r * RS:(r + 1) * RS], jnp.concatenate([keys(j)] * 2, axis=1))
        return jnp.where(causal, s, -jnp.inf) if j < 0 else s

    best, accum = [None] * parts, [None] * parts
    ahead = score(units[0])
    for i, (r, j) in enumerate(units):
        s = ahead
        if i + 1 < len(units):
            ahead = score(units[i + 1])
        top = jnp.max(s, axis=1, keepdims=True)
        if j < 0:
            best[r] = top
            accum[r] = pv(jnp.exp2(s - top).astype(BF16), values(j))
        else:
            new = jnp.maximum(best[r], top)
            p = jnp.exp2(s - new).astype(BF16)
            accum[r] = accum[r] * jnp.exp2(best[r] - new) + pv(p, values(j))
            best[r] = new
    keep = lax.broadcasted_iota(jnp.int32, (ROWS, HD), 0) < live
    for r in range(parts):
        out = accum[r][:, :HD] / accum[r][:, HD:]
        for h in range(RS // ROWS):
            n = r * (RS // ROWS) + h
            o_ref[:, n * HD:(n + 1) * HD] = jnp.where(keep, out[h * ROWS:(h + 1) * ROWS], 0.0).astype(BF16)


def attend_group(shifts, place, q_ref, sk_ref, sv_ref, k_ref, v_ref, out_refs):
    for shift, o_ref in zip(shifts, out_refs):
        t = lax.rem(place[1] + shift, 8)
        attend(t, place[3] - t * ROWS, q_ref, sk_ref, sv_ref, k_ref, v_ref, o_ref)


def first_kernel(shifts, hit_len, suffix_len, page_map, q_ref, sk_ref, sv_ref, buf_ref, place, k_ref, v_ref, *out_refs):
    request = lax.axis_index("dp") * 8 + lax.axis_index("cache")
    place[0] = request
    place[1] = lax.axis_index("tensor")
    place[2] = hit_len[request]
    place[3] = suffix_len[request]
    prepare(place, page_map, buf_ref, sk_ref, k_ref, v_ref)
    attend_group(shifts, place, q_ref, sk_ref, sv_ref, k_ref, v_ref, out_refs)


def later_kernel(shifts, place, q_ref, sk_ref, sv_ref, k_ref, v_ref, *refs):
    attend_group(shifts, place, q_ref, sk_ref, sv_ref, k_ref, v_ref, refs[-len(shifts):])


def gather_kernel(place, *refs):
    out_ref = refs[-1]
    rows = pl.ds(pl.multiple_of(pl.program_id(0) * (ROWS // 2), ROWS // 2), ROWS // 2)
    for block, shift in zip(refs, sum(GROUPS, ())):
        source = lax.rem(place[1] + 8 - shift, 8)
        out_ref[0, :, pl.ds(pl.multiple_of(source * WIDTH, WIDTH), WIDTH)] = block[rows, :]


def local(queries, suffix_keys, suffix_values, prefix_keys, prefix_values, hit_len, suffix_len, page_map):
    q = queries[0].reshape(8, ROWS, WIDTH)
    sk, sv = suffix_keys[0], suffix_values[0]
    packed = jnp.concatenate([prefix_keys[0], prefix_values[0]], axis=1)
    buf = lax.all_to_all(packed, DEVICES, split_axis=0, concat_axis=0, tiled=True)
    block = jax.ShapeDtypeStruct((ROWS, WIDTH), BF16)
    keys = [jax.ShapeDtypeStruct((KEYS, HD), BF16), jax.ShapeDtypeStruct((KEYS, 2 * HD), BF16)]
    place, k, v, *blocks = pl.pallas_call(
        functools.partial(first_kernel, GROUPS[0]),
        in_specs=[SMEM] * 3 + [VMEM] * 4,
        out_specs=[SMEM] + [VMEM] * (2 + len(GROUPS[0])),
        out_shape=[jax.ShapeDtypeStruct((4,), jnp.int32)] + keys + [block] * len(GROUPS[0]),
        compiler_params=PARAMS,
        name="attend_first",
    )(hit_len, suffix_len, page_map, q, sk, sv, buf)
    def send(blocks, shifts):
        return [
            lax.ppermute(x, "tensor", [(z, (z + d) % 8) for z in range(8)]) if d else x
            for x, d in zip(blocks, shifts)
        ]

    sent = [send(blocks, GROUPS[0])]
    for i, shifts in enumerate(GROUPS[1:]):
        arrived = sent[i - 1] if i else []
        if i == len(GROUPS) - 2:
            arrived = arrived[:1]
        blocks = pl.pallas_call(
            functools.partial(later_kernel, shifts),
            in_specs=[SMEM] + [VMEM] * 5 + [pl.BlockSpec(memory_space=pl.ANY)] * len(arrived),
            out_specs=[VMEM] * len(shifts),
            out_shape=[block] * len(shifts),
            compiler_params=PARAMS,
            name="attend_later",
        )(place, q, sk, sv, k, v, *arrived)
        sent.append(send(blocks, shifts))
    blocks = sum(sent, [])
    return pl.pallas_call(
        gather_kernel,
        grid=(2,),
        in_specs=[SMEM] + [VMEM] * 8,
        out_specs=pl.BlockSpec((1, ROWS // 2, 8 * WIDTH), lambda i: (0, i, 0)),
        out_shape=jax.ShapeDtypeStruct((1, ROWS, 8 * WIDTH), BF16),
        compiler_params=PARAMS,
        name="gather_blocks",
    )(place, *blocks)


def solution(mesh):
    placed = (
        P(DEVICES, None, "tensor"),
        P(DEVICES, None, "tensor"),
        P(DEVICES, None, "tensor"),
        P(DEVICES, None, None, "tensor"),
        P(DEVICES, None, None, "tensor"),
        P(),
        P(),
        P(),
    )
    return jax.shard_map(
        local, mesh=mesh, in_specs=placed, out_specs=P(DEVICES, "tensor", None), check_vma=False
    )
```
